32 devices in a mesh: img: 8 (over y, x, core), seq: 4 (over z).
Axes of the slice: x: 2, y: 2, z: 4, core: 2. Of those that a mesh axis runs over, the one named last changes fastest.
Arguments:
- tokens: bfloat16 [24, 1376, 1024], P('img', 'seq'), may hold values from -6 to 6
- cotangent: bfloat16 [24, 1376, 1024], P('img', 'seq'), may hold values from -6 to 6
- token_mask: int32 [24, 1376], P('img'), may hold values from 0 to 1, as said below
- slot_flags: int32 [24], P('img'), may hold values 0 or 1
- w_qkv: bfloat16 [1024, 3072], P('img'), may hold values from -0.1875 to 0.1875
- w_out: bfloat16 [1024, 1024], P('img'), may hold values from -3 to 3
- w_up: bfloat16 [1024, 4096], P('img'), may hold values from -0.1875 to 0.1875
- w_down: bfloat16 [4096, 1024], P('img'), may hold values from -0.09375 to 0.09375
- norm_gain: bfloat16 [2, 1024], P(None, 'img'), may hold values from 0.5 to 1.5
- norm_bias: bfloat16 [2, 1024], P(None, 'img'), may hold values from -1.796875 to 1.796875
- proj_bias: bfloat16 [4, 1024], P(None, 'img'), may hold values from -1.796875 to 1.796875
- up_bias: bfloat16 [4096], P('img'), may hold values from -1.796875 to 1.796875
- layer_scale: bfloat16 [2, 1024], P(None, 'img'), may hold values from 0.5 to 1.5
Outputs:
- output: bfloat16 [24, 1376, 1024], P('img', 'seq')
- grad_tokens: bfloat16 [24, 1376, 1024], P('img', 'seq')
- grad_w_qkv: float32 [1024, 3072], P('img')
- grad_w_out: float32 [1024, 1024], P('img')
- grad_w_up: float32 [1024, 4096], P('img')
- grad_w_down: float32 [4096, 1024], P('img')
- grad_norm_gain: float32 [2, 1024], P(None, 'img')
- grad_norm_bias: float32 [2, 1024], P(None, 'img')
- grad_proj_bias: float32 [4, 1024], P(None, 'img')
- grad_up_bias: float32 [4096], P('img')
- grad_layer_scale: float32 [2, 1024], P(None, 'img')
The draws below stay inside these ranges and needn't reach their ends.
Inputs may be any that keep to these rules, and one draw needn't show every extreme that they name: `token_mask`: each slot's real tokens are its first positions, at least 688 of them; some slot is full in every draw.
All inputs are finite; a program needn't handle non-finite values. No bound on the sum of `slot_flags` on one device may be relied on, other than what follows from the above.
Results may differ from the reference program's by a relative error of at most 0.018.
Values may be sent and summed in bfloat16 or wider, within the bound.
A program may use at most 320 MiB of HBM per device.

```python
import jax
import jax.numpy as jnp
from jax import lax

D = 1024
H = 16
HD = 64
FF = 4096
SEQ = 1376
SLOTS = 24


def draw_token_mask(key, part):
    key = jax.random.fold_in(key, 11)
    first, second = jax.random.split(key)
    lengths = jax.random.randint(first, (SLOTS,), SEQ // 2, SEQ + 1)
    chosen = jax.random.randint(second, (), 0, SLOTS)
    lengths = jnp.where(jnp.arange(SLOTS) == chosen, SEQ, lengths)
    return (jnp.arange(SEQ)[None, :] < lengths[:, None]).astype(jnp.int32)


def place_ends(entries, stream_key, smallest, high):
    longest = entries.shape.index(max(entries.shape))
    spots = []
    for shift in (0, 1):
        where = [jax.random.randint(jax.random.fold_in(stream_key, axis), (), 0, length) for axis, length in enumerate(entries.shape)]
        where[longest] = (where[longest] + shift) % entries.shape[longest]
        spots.append(tuple(where))
    return entries.at[spots[0]].set(smallest).at[spots[1]].set(high)


def levels(rng, dims, pieces, smallest, top_value):
    loudness, own = 1.0, jax.random.fold_in(rng, 6)
    for axis_at, parts in pieces:
        steps = jnp.exp(jax.random.uniform(jax.random.fold_in(own, axis_at), (parts,), jnp.float32, smallest / len(pieces), top_value / len(pieces)))
        loudness = loudness * jnp.repeat(steps, dims[axis_at] // parts).reshape([-1 if axis == axis_at else 1 for axis in range(len(dims))])
    return loudness


def noise(key, dims, width, reach, cuts=(), held_as=jnp.bfloat16):
    values = width * jax.random.normal(key, dims, jnp.float32)
    if cuts:
        values = values * levels(key, dims, cuts, -0.22, 0.18)
    return jnp.clip(values, -reach, reach).astype(held_as)


def setup_inputs(seed: int = 0) -> dict:
    streams_of = jax.random.split(jax.random.key(seed), 14)
    tokens = noise(streams_of[0], (SLOTS, SEQ, D), 1.0, 6.0, ((0, 8), (1, 4)))
    cotangent = noise(streams_of[1], (SLOTS, SEQ, D), 1.0, 6.0, ((0, 8), (1, 4)))
    token_mask = draw_token_mask(jax.random.fold_in(streams_of[13], 71), 0)
    slot_flags = place_ends((jax.random.randint(streams_of[3], (SLOTS,), 0, 16) < 13).astype(jnp.int32), jax.random.fold_in(streams_of[3], 1), 0, 1)
    w_qkv = noise(streams_of[4], (D, 3 * D), D ** -0.5, 0.1875, ((0, 8),))
    w_out = noise(streams_of[5], (D, D), 4 ** -0.5, 3.0, ((0, 8),))
    w_up = noise(streams_of[6], (D, FF), D ** -0.5, 0.1875, ((0, 8),))
    w_down = noise(streams_of[7], (FF, D), FF ** -0.5, 0.09375, ((0, 8),))
    norm_gain = jnp.clip(1.0 + 0.1 * jax.random.normal(streams_of[8], (2, D), jnp.float32), 0.5, 1.5).astype(jnp.bfloat16)
    norm_bias = noise(streams_of[9], (2, D), 0.3, 1.796875, ((1, 8),))
    proj_bias = noise(streams_of[10], (4, D), 0.3, 1.796875, ((1, 8),))
    up_bias = noise(streams_of[11], (FF,), 0.3, 1.796875, ((0, 8),))
    layer_scale = jnp.clip(0.5 + 1.0 * jax.random.uniform(streams_of[12], (2, D), jnp.float32) ** levels(streams_of[12], (2, D), ((1, 8),), -0.2, 0.2), 0.5, 1.5).astype(jnp.bfloat16)
    return {"tokens": tokens, "cotangent": cotangent, "token_mask": token_mask, "slot_flags": slot_flags, "w_qkv": w_qkv, "w_out": w_out, "w_up": w_up, "w_down": w_down, "norm_gain": norm_gain, "norm_bias": norm_bias, "proj_bias": proj_bias, "up_bias": up_bias, "layer_scale": layer_scale}


@jax.custom_vjp
def low(v):
    return lax.optimization_barrier(v.astype(jnp.bfloat16)).astype(jnp.float32)

@jax.custom_vjp
def low_back(v):
    return v

def low_keep(v):
    return (low(v), None)

def low_pass(kept, grad):
    return (grad,)

def back_keep(v):
    return (v, None)

def back_low(kept, grad):
    return (low(grad),)
low.defvjp(low_keep, low_pass)
low_back.defvjp(back_keep, back_low)
norm_eps = 1e-06

def norm_rows(values, gain, shift):
    center = values - lax.optimization_barrier(jnp.mean(values, axis=-1, keepdims=True))
    spread = lax.optimization_barrier(jnp.mean(center * center, axis=-1, keepdims=True))
    return center * lax.rsqrt(spread + norm_eps) * gain + shift

def product(left, right):
    return jnp.dot(left, right, precision=lax.Precision.HIGHEST)

def image_attention(block_item):
    queries, key_part, value_part, key_mask = block_item
    raw = jnp.einsum('qhd,khd->hqk', queries, key_part, precision=lax.Precision.HIGHEST) * HD ** (-0.5)
    scores = low_back(raw)
    scores = jnp.where(key_mask[None, None, :] > 0, scores, -1e+30)
    row_max = lax.optimization_barrier(jnp.max(scores, axis=-1, keepdims=True))
    weights_exp = jnp.exp(scores - row_max)
    probs = weights_exp / lax.optimization_barrier(jnp.sum(weights_exp, axis=-1, keepdims=True))
    return jnp.einsum('hqk,khd->qhd', low(probs), value_part, precision=lax.Precision.HIGHEST)

def layer(inputs, key_mask, live_rows, w_qkv, w_out, w_up, w_down, norm_gain, norm_bias, proj_bias, up_bias, layer_scale):
    group = inputs.shape[0]
    flat = inputs.reshape(-1, D)
    normed_one = low(norm_rows(flat, norm_gain[0], norm_bias[0]))
    shift_qkv = jnp.concatenate([proj_bias[0], jnp.zeros((D,), flat.dtype), proj_bias[1]])
    qkv = low_back(low(product(normed_one, w_qkv) + shift_qkv)).reshape(group, SEQ, 3, H, HD)
    checked = jax.checkpoint(image_attention)
    mixed = lax.map(checked, (qkv[:, :, 0], qkv[:, :, 1], qkv[:, :, 2], key_mask))
    attended = low_back(low(mixed)).reshape(-1, D)
    branch = low_back(product(attended, w_out) + proj_bias[2])
    middle = flat + layer_scale[0] * branch
    normed_two = low(norm_rows(middle, norm_gain[1], norm_bias[1]))
    up_proj = low_back(product(normed_two, w_up) + up_bias)
    activated = low(jax.nn.gelu(up_proj, approximate=False))
    down_proj = low_back(product(activated, w_down) + proj_bias[3])
    result = middle + layer_scale[1] * down_proj
    return result.reshape(group, SEQ, D) * live_rows

def reference(tokens, cotangent, token_mask, slot_flags, w_qkv, w_out, w_up, w_down, norm_gain, norm_bias, proj_bias, up_bias, layer_scale):
    params = tuple((p.astype(jnp.float32) for p in (w_qkv, w_out, w_up, w_down, norm_gain, norm_bias, proj_bias, up_bias, layer_scale)))
    pairs = SLOTS // 2
    live = (token_mask * slot_flags[:, None]).astype(jnp.float32)
    inputs = tokens.astype(jnp.float32).reshape(pairs, 2, SEQ, D)
    cotans = cotangent.astype(jnp.float32).reshape(pairs, 2, SEQ, D)
    masks = token_mask.reshape(pairs, 2, SEQ)
    lives = live.reshape(pairs, 2, SEQ, 1)

    def step(grad_total, block_item):
        block_in, block_cot, key_mask, live_rows = block_item

        def forward(values, *weights):
            return layer(values, key_mask, live_rows, *weights)
        result, pull = jax.vjp(forward, block_in, *params)
        grads = pull(block_cot)
        grad_total = tuple((a + b for a, b in zip(grad_total, grads[1:])))
        return (grad_total, (result.astype(jnp.bfloat16), grads[0].astype(jnp.bfloat16)))
    zero_grads = tuple((jnp.zeros_like(p) for p in params))
    grad_total, (results, grad_in) = lax.scan(step, zero_grads, (inputs, cotans, masks, lives))
    return (results.reshape(SLOTS, SEQ, D), grad_in.reshape(SLOTS, SEQ, D), grad_total[0], grad_total[1], grad_total[2], grad_total[3], grad_total[4], grad_total[5], grad_total[6], grad_total[7], grad_total[8])
```

```python
import jax
import jax.numpy as jnp
from jax import lax
from jax.experimental import pallas as pl
from jax.experimental.pallas import tpu as pltpu
from jax.sharding import Mesh
from jax.sharding import PartitionSpec as P

HD = 64
PAIR = 2 * HD


norm_eps = 1e-06


def norm_rows(values, gain, shift):
    center = values - jnp.mean(values, axis=-1, keepdims=True)
    spread = jnp.mean(center * center, axis=-1, keepdims=True)
    return center * lax.rsqrt(spread + norm_eps) * gain + shift


def gelu_and_slope(values):
    half = 0.5 + 0.5 * lax.erf(values * 0.5**0.5)
    slope = half + values * jnp.exp(-0.5 * values * values) * (0.5 / jnp.pi) ** 0.5
    return (values * half).astype(jnp.bfloat16), slope


def chunks_of(total):
    cuts = list(range(0, total, 512)) + [total]
    return [(cuts[n], cuts[n + 1] - cuts[n]) for n in range(len(cuts) - 1)]


def lane_of(rows):
    return lax.broadcasted_iota(jnp.int32, (rows, PAIR), 1)


def in_three(values):
    high = values.astype(jnp.bfloat16).astype(jnp.float32)
    rest = values - high
    mid = rest.astype(jnp.bfloat16).astype(jnp.float32)
    return high, mid, rest - mid


def dot_nt(left, right):
    return lax.dot_general(left, right, (((1,), (1,)), ((), ())), preferred_element_type=jnp.float32)


def attend_kernel(qkv_ref, bias_ref, out_ref, log_ref):
    seq_len, width = out_ref.shape
    lane = lane_of(seq_len)
    bias = jnp.broadcast_to(bias_ref[...], (seq_len, PAIR))
    ones = jnp.ones((seq_len, PAIR), jnp.bfloat16)
    key_extra = jnp.where(lane == 0, bias, 0.0).astype(jnp.bfloat16)
    for pair in range(width // PAIR):
        at = pair * PAIR
        keys = qkv_ref[:, 3 * at + PAIR : 3 * at + 2 * PAIR]
        values = qkv_ref[:, 3 * at + 2 * PAIR : 3 * at + 3 * PAIR]
        value_wide = jnp.concatenate([values, ones], axis=1)
        for start, size in chunks_of(seq_len):
            rows = slice(start, start + size)
            first = lane_of(size) < HD
            query = qkv_ref[rows, 3 * at : 3 * at + PAIR] * jnp.bfloat16(0.125)
            query_extra = jnp.where(lane_of(size) == 0, 1.0, 0.0).astype(jnp.bfloat16)
            query_wide = jnp.concatenate([query, query_extra], axis=1)
            parts = []
            for half in range(2):
                own = (lane >= HD) if half else (lane < HD)
                key_own = jnp.where(own, keys.astype(jnp.float32), 0.0).astype(jnp.bfloat16)
                key_wide = jnp.concatenate([key_own, key_extra], axis=1)
                scores = dot_nt(query_wide, key_wide)
                row_max = jnp.max(scores, axis=1, keepdims=True)
                weights = jnp.exp(scores - row_max).astype(jnp.bfloat16)
                mixed = jnp.dot(weights, value_wide, preferred_element_type=jnp.float32)
                total = mixed[:, PAIR:]
                parts.append((mixed[:, :PAIR] / total, row_max + jnp.log(total)))
            out_ref[rows, at : at + PAIR] = jnp.where(first, parts[0][0], parts[1][0]).astype(
                out_ref.dtype
            )
            log_ref[rows, at : at + PAIR] = jnp.where(first, parts[0][1], parts[1][1])


def attend_back_kernel(qkv_ref, bias_ref, log_ref, out_ref, grad_ref, dqkv_ref):
    seq_len = out_ref.shape[0]
    lane = lane_of(seq_len)
    place = lax.rem(lane, HD)
    bias = jnp.broadcast_to(bias_ref[...], (seq_len, PAIR))
    minus = jnp.where(place < 3, -1.0, 0.0)
    key_tail = jnp.where(place == 3, bias, minus)
    query = qkv_ref[:, :PAIR] * jnp.bfloat16(0.125)
    keys = qkv_ref[:, PAIR : 2 * PAIR].astype(jnp.float32)
    values = qkv_ref[:, 2 * PAIR :].astype(jnp.float32)
    grad = grad_ref[...]
    high, mid, low = in_three(log_ref[...])
    tail = jnp.where(place == 0, high, jnp.where(place == 1, mid, low))
    tail = jnp.where(place < 3, tail, jnp.where(place == 3, 1.0, 0.0))
    query_wide = jnp.concatenate([query, tail.astype(jnp.bfloat16)], axis=1)
    product = grad.astype(jnp.float32) * out_ref[...].astype(jnp.float32)
    inner_a = jnp.sum(jnp.where(lane < HD, product, 0.0), axis=1, keepdims=True)
    inner_b = jnp.sum(jnp.where(lane < HD, 0.0, product), axis=1, keepdims=True)
    high, mid, low = in_three(jnp.where(lane < HD, inner_a, inner_b))
    tail = jnp.where(place == 0, high, jnp.where(place == 1, mid, low))
    tail = jnp.where(place < 3, tail, 0.0)
    grad_wide = jnp.concatenate([grad, tail.astype(jnp.bfloat16)], axis=1)
    total_q = [None, None]
    for start, size in chunks_of(seq_len):
        rows = slice(start, start + size)
        first = lane_of(size) < HD
        keys_here = keys[rows].astype(jnp.bfloat16)
        parts = []
        for half in range(2):
            own = jnp.logical_not(first) if half else first
            key_wide = jnp.concatenate(
                [jnp.where(own, keys[rows], 0.0), jnp.where(own, key_tail[rows], 0.0)], axis=1
            ).astype(jnp.bfloat16)
            value_wide = jnp.concatenate(
                [jnp.where(own, values[rows], 0.0), jnp.where(own, minus[rows], 0.0)], axis=1
            ).astype(jnp.bfloat16)
            probs = jnp.exp(dot_nt(key_wide, query_wide))
            grad_scores = (probs * dot_nt(value_wide, grad_wide)).astype(jnp.bfloat16)
            grad_value = jnp.dot(
                probs.astype(jnp.bfloat16), grad, preferred_element_type=jnp.float32
            )
            grad_key = jnp.dot(grad_scores, query, preferred_element_type=jnp.float32)
            part_q = lax.dot_general(
                grad_scores,
                keys_here,
                (((0,), (0,)), ((), ())),
                preferred_element_type=jnp.float32,
            )
            total_q[half] = part_q if total_q[half] is None else total_q[half] + part_q
            parts.append((grad_key, grad_value))
        dqkv_ref[rows, PAIR : 2 * PAIR] = jnp.where(first, parts[0][0], parts[1][0]).astype(
            dqkv_ref.dtype
        )
        dqkv_ref[rows, 2 * PAIR :] = jnp.where(first, parts[0][1], parts[1][1]).astype(
            dqkv_ref.dtype
        )
    dqkv_ref[:, :PAIR] = (jnp.where(lane < HD, total_q[0], total_q[1]) * 0.125).astype(
        dqkv_ref.dtype
    )


def attend(qkv, key_bias):
    seq_len, triple = qkv.shape
    width = triple // 3
    return pl.pallas_call(
        attend_kernel,
        out_shape=(
            jax.ShapeDtypeStruct((seq_len, width), jnp.bfloat16),
            jax.ShapeDtypeStruct((seq_len, width), jnp.float32),
        ),
        cost_estimate=pl.CostEstimate(
            flops=16 * seq_len * seq_len * width,
            bytes_accessed=14 * seq_len * width,
            transcendentals=seq_len * seq_len * width // HD,
        ),
        compiler_params=pltpu.CompilerParams(vmem_limit_bytes=48 * 1024 * 1024),
        name="attend",
    )(qkv, key_bias)


def attend_back(pair, qkv, key_bias, log_total, mixed, grad_mixed):
    seq_len = qkv.shape[0]
    one = pl.BlockSpec((seq_len, PAIR), lambda i: (0, pair))
    return pl.pallas_call(
        attend_back_kernel,
        grid=(1,),
        in_specs=[
            pl.BlockSpec((seq_len, 3 * PAIR), lambda i: (0, pair)),
            pl.BlockSpec((seq_len, 1), lambda i: (0, 0)),
            one,
            one,
            one,
        ],
        out_specs=pl.BlockSpec((seq_len, 3 * PAIR), lambda i: (0, 0)),
        out_shape=jax.ShapeDtypeStruct((seq_len, 3 * PAIR), jnp.bfloat16),
        cost_estimate=pl.CostEstimate(
            flops=40 * seq_len * seq_len * PAIR,
            bytes_accessed=20 * seq_len * PAIR,
            transcendentals=seq_len * seq_len * PAIR // HD,
        ),
        compiler_params=pltpu.CompilerParams(vmem_limit_bytes=48 * 1024 * 1024),
        name="attend_back",
    )(qkv, key_bias, log_total, mixed, grad_mixed)


HOME = ("core", "low")
IMG = ("chip", "core")
SEQ = ("high", "low")


def traded(values):
    moved = lax.ppermute(values, ("core", "high"), [(1, 2), (2, 1)])
    return jnp.where(lax.axis_index("core") == lax.axis_index("high"), values, moved)


def swapped(values, axis, bit=1):
    count = lax.axis_size(axis)
    return lax.ppermute(values, axis, [(n, n ^ bit) for n in range(count)])


def summed(values):
    for axis in ("core", "low", "chip", "high"):
        bit = 1
        while bit < lax.axis_size(axis):
            values = values + swapped(values, axis, bit)
            bit *= 2
    return values


def summed_seq(values):
    if lax.axis_size("low") != 2:
        return lax.psum(values, SEQ).astype(jnp.float32)
    rows = values.shape[0] // 2
    low = lax.axis_index("low")
    mine = lax.dynamic_slice_in_dim(values, low * rows, rows, 0)
    other = lax.dynamic_slice_in_dim(values, (1 - low) * rows, rows, 0)
    mine = mine + swapped(other, "low")
    mine = mine + swapped(mine, "high")
    other = swapped(mine, "low")
    first = jnp.where(low == 0, mine, other)
    second = jnp.where(low == 0, other, mine)
    return jnp.concatenate([first, second], axis=0).astype(jnp.float32)


def rows_of(left):
    chips = lax.axis_size("chip")
    chip, core = lax.axis_index("chip"), lax.axis_index("core")
    part = left.shape[1] // (2 * chips)

    def side_of(side):
        order = [chip ^ (1 + side), chip ^ 3, chip ^ (2 - side), chip]
        order = order if chips == 4 else range(chips)
        picked = [lax.dynamic_slice_in_dim(left, (n * 2 + side) * part, part, 1) for n in order]
        return jnp.concatenate(picked, axis=1)

    return lax.optimization_barrier((side_of(1 - core), side_of(core)))


def product(left, right):
    return lax.dot_general(
        left, right, (((0,), (0,)), ((), ())), preferred_element_type=jnp.float32
    ).astype(jnp.bfloat16)


def products(rows, right):
    return product(rows[0], right), product(rows[1], right)


def owned(send, keep):
    chips = lax.axis_size("chip")
    total = keep + swapped(send, "core")
    if chips != 4:
        total = lax.psum_scatter(total, "chip", scatter_dimension=0, tiled=True)
        return summed_seq(total)
    total = total.reshape(chips, -1, total.shape[1])
    first = [(n * 2 + c, (n ^ (1 + c)) * 2 + c) for n in range(chips) for c in range(2)]
    second = [(n * 2 + c, (n ^ (2 - c)) * 2 + c) for n in range(chips) for c in range(2)]
    came = lax.ppermute(total[:2], IMG, first)
    onward = total[2] + came[1]
    total = total[3] + came[0] + lax.ppermute(onward, IMG, second)
    return summed_seq(total)


def body(
    tokens,
    cotangent,
    token_mask,
    slot_flags,
    w_qkv,
    w_out,
    w_up,
    w_down,
    norm_gain,
    norm_bias,
    proj_bias,
    up_bias,
    layer_scale,
):
    seq_count = lax.axis_size(HOME)
    seq_place = lax.axis_index(HOME)
    img_count = lax.axis_size(IMG)
    img_place = lax.axis_index(IMG)
    images, local_rows, model_width = tokens.shape
    seq_len = token_mask.shape[1]
    head_cols = model_width // seq_count
    pairs = head_cols // PAIR
    shard = norm_gain.shape[1]
    up_rows = up_bias.shape[0] // shard

    facts = traded(jnp.concatenate([jnp.sum(token_mask, axis=1), slot_flags]))
    lengths, flags = facts[:images], facts[images:]
    here = lax.broadcasted_iota(jnp.int32, (images, local_rows), 1) + seq_place * local_rows
    live_rows = ((here < lengths[:, None]) & (flags[:, None] > 0)).astype(jnp.float32)
    live_rows = live_rows.reshape(-1, 1)
    place = lax.broadcasted_iota(jnp.int32, (images, seq_len, 1), 1)
    place = place + ((place // local_rows) ^ seq_place) * local_rows - place // local_rows * local_rows
    key_bias = jnp.where(place < lengths[:, None, None], 0.0, -1e30).astype(jnp.float32)

    def by_pair(matrix):
        rows = matrix.shape[0]
        split = matrix.reshape(rows, 3, seq_count, pairs, PAIR)
        return split.transpose(0, 3, 2, 1, 4).reshape(rows, -1)

    def by_kind(matrix):
        rows = matrix.shape[0]
        split = matrix.reshape(rows, pairs, seq_count, 3, PAIR)
        return split.transpose(0, 3, 2, 1, 4).reshape(rows, -1)

    def to_heads(matrix, runs=1):
        width = matrix.shape[1] // (seq_count * runs)
        parts = []
        for n in range(seq_count):
            part = [
                lax.dynamic_slice_in_dim(
                    matrix, (run * seq_count + (seq_place ^ n)) * width, width, 1
                )
                for run in range(runs)
            ]
            part = jnp.concatenate(part, axis=1)
            parts.append(swapped(part, HOME, n) if n else part)
        return jnp.concatenate(parts, axis=0)

    def to_tokens(block):
        parts = []
        for n in range(seq_count):
            part = block[n * local_rows : (n + 1) * local_rows]
            parts.append(swapped(part, HOME, n) if n else part)
        return parts

    def laid(slots):
        width = slots[0][0].shape[1]
        whole = jnp.zeros((images * local_rows, seq_count * width), jnp.bfloat16)
        for slot, parts in enumerate(slots):
            for n, part in enumerate(parts):
                whole = lax.dynamic_update_slice(
                    whole, part, (slot * local_rows, (seq_place ^ n) * width)
                )
        return whole

    small = jnp.concatenate(
        [norm_gain, norm_bias, proj_bias, layer_scale, up_bias.reshape(up_rows, shard)], axis=0
    )
    small = lax.all_gather(small, IMG, axis=0, tiled=False).astype(jnp.float32)
    up_bias_f = small[:, 10:].reshape(-1)
    small = small.swapaxes(0, 1).reshape(-1, model_width)
    gain_f, shift_f, bias_f, scale_f = (small[0:2], small[2:4], small[4:8], small[8:10])
    qkv_full = lax.all_gather(by_pair(w_qkv), IMG, axis=0, tiled=True)
    out_full = lax.all_gather(w_out, IMG, axis=0, tiled=True)
    up_full = lax.all_gather(w_up, IMG, axis=0, tiled=True)
    down_full = lax.all_gather(w_down, IMG, axis=0, tiled=True)

    tokens = jnp.stack([traded(tokens[slot]) for slot in range(images)])
    inputs = tokens.reshape(-1, model_width).astype(jnp.float32)
    normed_one, norm_one_pulls = [], []
    for slot in range(images):
        normed, pull = jax.vjp(norm_rows, tokens[slot].astype(jnp.float32), gain_f[0], shift_f[0])
        normed_one.append(normed.astype(jnp.bfloat16))
        norm_one_pulls.append(pull)
    rows_one = rows_of(jnp.concatenate(normed_one, axis=0))
    shift_qkv = jnp.concatenate([bias_f[0], jnp.zeros((model_width,), jnp.float32), bias_f[1]])
    shift_qkv = by_pair(shift_qkv[None])
    saved = []
    returned = []
    for slot in range(images):
        qkv = jnp.dot(normed_one[slot], qkv_full, preferred_element_type=jnp.float32)
        qkv = (qkv + shift_qkv).astype(jnp.bfloat16)
        spread = to_heads(qkv, pairs)
        mixed, log_total = attend(spread, key_bias[slot])
        saved.append((spread, key_bias[slot], log_total, mixed))
        returned.append(to_tokens(mixed))
    last, cotangent = lax.optimization_barrier((saved[-1][0], cotangent))
    saved[-1] = (last,) + saved[-1][1:]
    cotangent = traded(cotangent)
    attended = laid(returned)
    branch = jnp.dot(attended, out_full, preferred_element_type=jnp.float32) + bias_f[2]
    middle = inputs + scale_f[0] * branch
    normed_two, norm_two_pull = jax.vjp(norm_rows, middle, gain_f[1], shift_f[1])
    normed_two = normed_two.astype(jnp.bfloat16)
    up_proj = jnp.dot(normed_two, up_full, preferred_element_type=jnp.float32) + up_bias_f
    activated, gelu_slope = lax.optimization_barrier(gelu_and_slope(up_proj))
    grad_y = cotangent.reshape(-1, model_width).astype(jnp.float32) * live_rows
    grad_down = (grad_y * scale_f[1]).astype(jnp.bfloat16)
    grad_bias_down = jnp.sum(grad_down.astype(jnp.float32), axis=0)
    barrier = lax.optimization_barrier
    grad_down, grad_w_down = barrier((grad_down, product(activated, grad_down)))
    grad_w_down = lax.psum_scatter(grad_w_down, IMG, scatter_dimension=0, tiled=True)
    grad_act = jnp.dot(grad_down, down_full.T, preferred_element_type=jnp.float32)
    grad_up = (grad_act * gelu_slope).astype(jnp.bfloat16)
    grad_up_bias = jnp.sum(grad_up.astype(jnp.float32), axis=0)
    grad_up, grad_w_up = barrier((grad_up, product(normed_two, grad_up)))
    grad_w_up = lax.psum_scatter(grad_w_up, IMG, scatter_dimension=0, tiled=True)
    grad_normed_two = jnp.dot(grad_up, up_full.T, preferred_element_type=jnp.float32)
    grad_from_two, grad_gain_two, grad_shift_two = norm_two_pull(grad_normed_two)
    grad_middle = grad_y + grad_from_two
    grad_scale_one = jnp.sum(grad_middle * branch, axis=0)
    grad_branch = (grad_middle * scale_f[0]).astype(jnp.bfloat16)
    grad_bias_out = jnp.sum(grad_branch.astype(jnp.float32), axis=0)
    grad_attended = jnp.dot(grad_branch, out_full.T, preferred_element_type=jnp.float32).astype(
        jnp.bfloat16
    )
    grad_attended = grad_attended.reshape(images, local_rows, model_width)

    grad_w_out = products(rows_of(attended), grad_branch)
    grads_mixed = [to_heads(grad_attended[slot]) for slot in range(images)]
    grad_parts = []
    grad_w_qkv = []
    for pair in range(pairs):
        grad_slots = []
        for slot in range(images):
            spread, slot_bias, log_total, mixed = saved[slot]
            if pair == 0 and slot == 0:
                spread, grad_w_out = barrier((spread, grad_w_out))
            if pair and slot == images - 1:
                earlier = barrier((grad_parts[-1], grad_slots))
                grad_parts[-1] = laid(earlier[0])
                grad_slots = earlier[1]
                grad_w_qkv.append(products(rows_one, grad_parts[-1]))
                spread, grad_w_qkv[-1] = barrier((spread, grad_w_qkv[-1]))
            last = attend_back(pair, spread, slot_bias, log_total, mixed, grads_mixed[slot])
            if slot == images - 1 and pair == pairs - 1:
                last, activated = barrier((last, activated))
            grad_slots.append(to_tokens(last))
        grad_parts.append(grad_slots)
    grad_parts[-1] = laid(grad_parts[-1])
    grad_w_qkv.append(products(rows_one, grad_parts[-1]))
    grad_w_down, grad_w_up = (
        grad.astype(jnp.float32) for grad in lax.psum((grad_w_down, grad_w_up), SEQ)
    )
    grad_w_qkv[0] = [
        jnp.concatenate(both, axis=1) for both in zip(grad_w_qkv[0], grad_w_out, strict=True)
    ]
    grad_w_qkv = jnp.concatenate([owned(*both) for both in grad_w_qkv], axis=1)
    cut = 3 * seq_count * PAIR
    grad_w_out = grad_w_qkv[:, cut : cut + model_width]
    grad_w_qkv = jnp.concatenate([grad_w_qkv[:, :cut], grad_w_qkv[:, cut + model_width :]], axis=1)
    grad_w_qkv = by_kind(grad_w_qkv)

    down_proj = jnp.dot(activated, down_full, preferred_element_type=jnp.float32) + bias_f[3]
    result = (
        ((middle + scale_f[1] * down_proj) * live_rows).astype(jnp.bfloat16).reshape(tokens.shape)
    )
    result = traded(result)
    grad_scale_two = jnp.sum(grad_y * down_proj, axis=0)
    grad_inputs, grad_gain_one, grad_shift_one = [], 0.0, 0.0
    for slot in range(images):
        rows = slice(slot * local_rows, (slot + 1) * local_rows)
        grad_normed = 0.0
        for pair in range(pairs):
            cols = slice(pair * seq_count * 3 * PAIR, (pair + 1) * seq_count * 3 * PAIR)
            grad_normed += lax.dot_general(
                grad_parts[pair][rows],
                qkv_full[:, cols],
                (((1,), (1,)), ((), ())),
                preferred_element_type=jnp.float32,
            )
        grad_from_one, grad_gain, grad_shift = norm_one_pulls[slot](grad_normed)
        grad_inputs.append(traded((grad_middle[rows] + grad_from_one).astype(jnp.bfloat16)))
        grad_gain_one += grad_gain
        grad_shift_one += grad_shift
    grad_inputs = jnp.stack(grad_inputs)
    grad_bias_qkv = [jnp.sum(part.astype(jnp.float32), axis=0) for part in grad_parts]
    grad_bias_qkv = by_kind(jnp.concatenate(grad_bias_qkv)[None])[0]
    smalls = jnp.stack(
        [
            grad_gain_one,
            grad_gain_two,
            grad_shift_one,
            grad_shift_two,
            grad_bias_qkv[:model_width],
            grad_bias_qkv[2 * model_width :],
            grad_bias_out,
            grad_bias_down,
            grad_scale_one,
            grad_scale_two,
        ]
    )
    grad_up_bias = grad_up_bias.reshape(img_count, up_rows, shard).swapaxes(0, 1)
    smalls = jnp.concatenate([smalls, grad_up_bias.reshape(up_rows, model_width)], axis=0)
    smalls = summed(smalls)
    smalls = lax.dynamic_slice_in_dim(smalls, img_place * shard, shard, 1)
    return (
        result,
        grad_inputs,
        grad_w_qkv,
        grad_w_out,
        grad_w_up,
        grad_w_down,
        smalls[0:2],
        smalls[2:4],
        smalls[4:8],
        smalls[10:].reshape(-1),
        smalls[8:10],
    )


def solution(mesh):
    img_count, seq_count = mesh.devices.shape
    split = mesh.devices.reshape(img_count // 2, 2, 2, seq_count // 2)
    mesh = Mesh(split, IMG + SEQ)
    placed = (
        P(IMG, SEQ, None),
        P(IMG, SEQ, None),
        P(IMG, None),
        P(IMG),
        P(IMG, None),
        P(IMG, None),
        P(IMG, None),
        P(IMG, None),
        P(None, IMG),
        P(None, IMG),
        P(None, IMG),
        P(IMG),
        P(None, IMG),
    )
    return jax.shard_map(
        body,
        mesh=mesh,
        in_specs=placed,
        out_specs=(
            P(IMG, SEQ, None),
            P(IMG, SEQ, None),
            P(IMG, None),
            P(IMG, None),
            P(IMG, None),
            P(IMG, None),
            P(None, IMG),
            P(None, IMG),
            P(None, IMG),
            P(IMG),
            P(None, IMG),
        ),
        check_vma=False,
    )
```

```python
import jax
import jax.numpy as jnp
from jax import lax
from jax.experimental import pallas as pl
from jax.experimental.pallas import tpu as pltpu
from jax.sharding import Mesh
from jax.sharding import PartitionSpec as P

HD = 64
PAIR = 2 * HD


norm_eps = 1e-06


def norm_rows(values, gain, shift):
    center = values - jnp.mean(values, axis=-1, keepdims=True)
    spread = jnp.mean(center * center, axis=-1, keepdims=True)
    return center * lax.rsqrt(spread + norm_eps) * gain + shift


def gelu_and_slope(values):
    half = 0.5 + 0.5 * lax.erf(values * 0.5**0.5)
    slope = half + values * jnp.exp(-0.5 * values * values) * (0.5 / jnp.pi) ** 0.5
    return (values * half).astype(jnp.bfloat16), slope


def chunks_of(total):
    cuts = list(range(0, total, 512)) + [total]
    return [(cuts[n], cuts[n + 1] - cuts[n]) for n in range(len(cuts) - 1)]


def lane_of(rows):
    return lax.broadcasted_iota(jnp.int32, (rows, PAIR), 1)


def in_three(values):
    high = values.astype(jnp.bfloat16).astype(jnp.float32)
    rest = values - high
    mid = rest.astype(jnp.bfloat16).astype(jnp.float32)
    return high, mid, rest - mid


def dot_nt(left, right):
    return lax.dot_general(left, right, (((1,), (1,)), ((), ())), preferred_element_type=jnp.float32)


def attend_kernel(qkv_ref, bias_ref, out_ref, log_ref):
    seq_len, width = out_ref.shape
    lane = lane_of(seq_len)
    bias = jnp.broadcast_to(bias_ref[...], (seq_len, PAIR))
    ones = jnp.ones((seq_len, PAIR), jnp.bfloat16)
    key_extra = jnp.where(lane == 0, bias, 0.0).astype(jnp.bfloat16)
    for pair in range(width // PAIR):
        at = pair * PAIR
        keys = qkv_ref[:, 3 * at + PAIR : 3 * at + 2 * PAIR]
        values = qkv_ref[:, 3 * at + 2 * PAIR : 3 * at + 3 * PAIR]
        value_wide = jnp.concatenate([values, ones], axis=1)
        for start, size in chunks_of(seq_len):
            rows = slice(start, start + size)
            first = lane_of(size) < HD
            query = qkv_ref[rows, 3 * at : 3 * at + PAIR] * jnp.bfloat16(0.125)
            query_extra = jnp.where(lane_of(size) == 0, 1.0, 0.0).astype(jnp.bfloat16)
            query_wide = jnp.concatenate([query, query_extra], axis=1)
            parts = []
            for half in range(2):
                own = (lane >= HD) if half else (lane < HD)
                key_own = jnp.where(own, keys.astype(jnp.float32), 0.0).astype(jnp.bfloat16)
                key_wide = jnp.concatenate([key_own, key_extra], axis=1)
                scores = dot_nt(query_wide, key_wide)
                row_max = jnp.max(scores, axis=1, keepdims=True)
                weights = jnp.exp(scores - row_max).astype(jnp.bfloat16)
                mixed = jnp.dot(weights, value_wide, preferred_element_type=jnp.float32)
                total = mixed[:, PAIR:]
                parts.append((mixed[:, :PAIR] / total, row_max + jnp.log(total)))
            out_ref[rows, at : at + PAIR] = jnp.where(first, parts[0][0], parts[1][0]).astype(
                out_ref.dtype
            )
            log_ref[rows, at : at + PAIR] = jnp.where(first, parts[0][1], parts[1][1])


def attend_back_kernel(qkv_ref, bias_ref, log_ref, out_ref, grad_ref, dqkv_ref):
    seq_len = out_ref.shape[0]
    lane = lane_of(seq_len)
    place = lax.rem(lane, HD)
    bias = jnp.broadcast_to(bias_ref[...], (seq_len, PAIR))
    minus = jnp.where(place < 3, -1.0, 0.0)
    key_tail = jnp.where(place == 3, bias, minus)
    query = qkv_ref[:, :PAIR] * jnp.bfloat16(0.125)
    keys = qkv_ref[:, PAIR : 2 * PAIR].astype(jnp.float32)
    values = qkv_ref[:, 2 * PAIR :].astype(jnp.float32)
    grad = grad_ref[...]
    high, mid, low = in_three(log_ref[...])
    tail = jnp.where(place == 0, high, jnp.where(place == 1, mid, low))
    tail = jnp.where(place < 3, tail, jnp.where(place == 3, 1.0, 0.0))
    query_wide = jnp.concatenate([query, tail.astype(jnp.bfloat16)], axis=1)
    product = grad.astype(jnp.float32) * out_ref[...].astype(jnp.float32)
    inner_a = jnp.sum(jnp.where(lane < HD, product, 0.0), axis=1, keepdims=True)
    inner_b = jnp.sum(jnp.where(lane < HD, 0.0, product), axis=1, keepdims=True)
    high, mid, low = in_three(jnp.where(lane < HD, inner_a, inner_b))
    tail = jnp.where(place == 0, high, jnp.where(place == 1, mid, low))
    tail = jnp.where(place < 3, tail, 0.0)
    grad_wide = jnp.concatenate([grad, tail.astype(jnp.bfloat16)], axis=1)
    total_q = [None, None]
    for start, size in chunks_of(seq_len):
        rows = slice(start, start + size)
        first = lane_of(size) < HD
        keys_here = keys[rows].astype(jnp.bfloat16)
        parts = []
        for half in range(2):
            own = jnp.logical_not(first) if half else first
            key_wide = jnp.concatenate(
                [jnp.where(own, keys[rows], 0.0), jnp.where(own, key_tail[rows], 0.0)], axis=1
            ).astype(jnp.bfloat16)
            value_wide = jnp.concatenate(
                [jnp.where(own, values[rows], 0.0), jnp.where(own, minus[rows], 0.0)], axis=1
            ).astype(jnp.bfloat16)
            probs = jnp.exp(dot_nt(key_wide, query_wide))
            grad_scores = (probs * dot_nt(value_wide, grad_wide)).astype(jnp.bfloat16)
            grad_value = jnp.dot(
                probs.astype(jnp.bfloat16), grad, preferred_element_type=jnp.float32
            )
            grad_key = jnp.dot(grad_scores, query, preferred_element_type=jnp.float32)
            part_q = lax.dot_general(
                grad_scores,
                keys_here,
                (((0,), (0,)), ((), ())),
                preferred_element_type=jnp.float32,
            )
            total_q[half] = part_q if total_q[half] is None else total_q[half] + part_q
            parts.append((grad_key, grad_value))
        dqkv_ref[rows, PAIR : 2 * PAIR] = jnp.where(first, parts[0][0], parts[1][0]).astype(
            dqkv_ref.dtype
        )
        dqkv_ref[rows, 2 * PAIR :] = jnp.where(first, parts[0][1], parts[1][1]).astype(
            dqkv_ref.dtype
        )
    dqkv_ref[:, :PAIR] = (jnp.where(lane < HD, total_q[0], total_q[1]) * 0.125).astype(
        dqkv_ref.dtype
    )


def attend(qkv, key_bias):
    seq_len, triple = qkv.shape
    width = triple // 3
    return pl.pallas_call(
        attend_kernel,
        out_shape=(
            jax.ShapeDtypeStruct((seq_len, width), jnp.bfloat16),
            jax.ShapeDtypeStruct((seq_len, width), jnp.float32),
        ),
        cost_estimate=pl.CostEstimate(
            flops=16 * seq_len * seq_len * width,
            bytes_accessed=14 * seq_len * width,
            transcendentals=seq_len * seq_len * width // HD,
        ),
        compiler_params=pltpu.CompilerParams(vmem_limit_bytes=48 * 1024 * 1024),
        name="attend",
    )(qkv, key_bias)


def attend_back(pair, qkv, key_bias, log_total, mixed, grad_mixed):
    seq_len = qkv.shape[0]
    one = pl.BlockSpec((seq_len, PAIR), lambda i: (0, pair))
    return pl.pallas_call(
        attend_back_kernel,
        grid=(1,),
        in_specs=[
            pl.BlockSpec((seq_len, 3 * PAIR), lambda i: (0, pair)),
            pl.BlockSpec((seq_len, 1), lambda i: (0, 0)),
            one,
            one,
            one,
        ],
        out_specs=pl.BlockSpec((seq_len, 3 * PAIR), lambda i: (0, 0)),
        out_shape=jax.ShapeDtypeStruct((seq_len, 3 * PAIR), jnp.bfloat16),
        cost_estimate=pl.CostEstimate(
            flops=40 * seq_len * seq_len * PAIR,
            bytes_accessed=20 * seq_len * PAIR,
            transcendentals=seq_len * seq_len * PAIR // HD,
        ),
        compiler_params=pltpu.CompilerParams(vmem_limit_bytes=48 * 1024 * 1024),
        name="attend_back",
    )(qkv, key_bias, log_total, mixed, grad_mixed)


HOME = ("core", "low")
IMG = ("chip", "core")
SEQ = ("high", "low")


def traded(values):
    moved = lax.ppermute(values, ("core", "high"), [(1, 2), (2, 1)])
    return jnp.where(lax.axis_index("core") == lax.axis_index("high"), values, moved)


def swapped(values, axis, bit=1):
    count = lax.axis_size(axis)
    return lax.ppermute(values, axis, [(n, n ^ bit) for n in range(count)])


def summed(values):
    for axis in ("core", "low", "chip", "high"):
        bit = 1
        while bit < lax.axis_size(axis):
            values = values + swapped(values, axis, bit)
            bit *= 2
    return values


def summed_seq(values):
    if lax.axis_size("low") != 2:
        return lax.psum(values, SEQ).astype(jnp.float32)
    rows = values.shape[0] // 2
    low = lax.axis_index("low")
    mine = lax.dynamic_slice_in_dim(values, low * rows, rows, 0)
    other = lax.dynamic_slice_in_dim(values, (1 - low) * rows, rows, 0)
    mine = mine + swapped(other, "low")
    mine = mine + swapped(mine, "high")
    other = swapped(mine, "low")
    first = jnp.where(low == 0, mine, other)
    second = jnp.where(low == 0, other, mine)
    return jnp.concatenate([first, second], axis=0).astype(jnp.float32)


def rows_of(left):
    chips = lax.axis_size("chip")
    chip, core = lax.axis_index("chip"), lax.axis_index("core")
    part = left.shape[1] // (2 * chips)

    def side_of(side):
        order = [chip ^ (1 + side), chip ^ 3, chip ^ (2 - side), chip]
        order = order if chips == 4 else range(chips)
        picked = [lax.dynamic_slice_in_dim(left, (n * 2 + side) * part, part, 1) for n in order]
        return jnp.concatenate(picked, axis=1)

    return lax.optimization_barrier((side_of(1 - core), side_of(core)))


def product(left, right):
    return lax.dot_general(
        left, right, (((0,), (0,)), ((), ())), preferred_element_type=jnp.float32
    ).astype(jnp.bfloat16)


def products(rows, right):
    return product(rows[0], right), product(rows[1], right)


def owned(send, keep):
    chips = lax.axis_size("chip")
    total = keep + swapped(send, "core")
    if chips != 4:
        total = lax.psum_scatter(total, "chip", scatter_dimension=0, tiled=True)
        return summed_seq(total)
    total = total.reshape(chips, -1, total.shape[1])
    first = [(n * 2 + c, (n ^ (1 + c)) * 2 + c) for n in range(chips) for c in range(2)]
    second = [(n * 2 + c, (n ^ (2 - c)) * 2 + c) for n in range(chips) for c in range(2)]
    came = lax.ppermute(total[:2], IMG, first)
    onward = total[2] + came[1]
    total = total[3] + came[0] + lax.ppermute(onward, IMG, second)
    return summed_seq(total)


def body(
    tokens,
    cotangent,
    token_mask,
    slot_flags,
    w_qkv,
    w_out,
    w_up,
    w_down,
    norm_gain,
    norm_bias,
    proj_bias,
    up_bias,
    layer_scale,
):
    seq_count = lax.axis_size(HOME)
    seq_place = lax.axis_index(HOME)
    img_count = lax.axis_size(IMG)
    img_place = lax.axis_index(IMG)
    images, local_rows, model_width = tokens.shape
    seq_len = token_mask.shape[1]
    head_cols = model_width // seq_count
    pairs = head_cols // PAIR
    shard = norm_gain.shape[1]
    up_rows = up_bias.shape[0] // shard

    facts = traded(jnp.concatenate([jnp.sum(token_mask, axis=1), slot_flags]))
    lengths, flags = facts[:images], facts[images:]
    here = lax.broadcasted_iota(jnp.int32, (images, local_rows), 1) + seq_place * local_rows
    live_rows = ((here < lengths[:, None]) & (flags[:, None] > 0)).astype(jnp.float32)
    live_rows = live_rows.reshape(-1, 1)
    place = lax.broadcasted_iota(jnp.int32, (images, seq_len, 1), 1)
    place = place + ((place // local_rows) ^ seq_place) * local_rows - place // local_rows * local_rows
    key_bias = jnp.where(place < lengths[:, None, None], 0.0, -1e30).astype(jnp.float32)

    def by_pair(matrix):
        rows = matrix.shape[0]
        split = matrix.reshape(rows, 3, seq_count, pairs, PAIR)
        return split.transpose(0, 3, 2, 1, 4).reshape(rows, -1)

    def by_kind(matrix):
        rows = matrix.shape[0]
        split = matrix.reshape(rows, pairs, seq_count, 3, PAIR)
        return split.transpose(0, 3, 2, 1, 4).reshape(rows, -1)

    def to_heads(matrix, runs=1):
        width = matrix.shape[1] // (seq_count * runs)
        parts = []
        for n in range(seq_count):
            part = [
                lax.dynamic_slice_in_dim(
                    matrix, (run * seq_count + (seq_place ^ n)) * width, width, 1
                )
                for run in range(runs)
            ]
            part = jnp.concatenate(part, axis=1)
            parts.append(swapped(part, HOME, n) if n else part)
        return jnp.concatenate(parts, axis=0)

    def to_tokens(block):
        parts = []
        for n in range(seq_count):
            part = block[n * local_rows : (n + 1) * local_rows]
            parts.append(swapped(part, HOME, n) if n else part)
        return parts

    def laid(slots):
        width = slots[0][0].shape[1]
        whole = jnp.zeros((images * local_rows, seq_count * width), jnp.bfloat16)
        for slot, parts in enumerate(slots):
            for n, part in enumerate(parts):
                whole = lax.dynamic_update_slice(
                    whole, part, (slot * local_rows, (seq_place ^ n) * width)
                )
        return whole

    small = jnp.concatenate(
        [norm_gain, norm_bias, proj_bias, layer_scale, up_bias.reshape(up_rows, shard)], axis=0
    )
    small = lax.all_gather(small, IMG, axis=0, tiled=False).astype(jnp.float32)
    up_bias_f = small[:, 10:].reshape(-1)
    small = small.swapaxes(0, 1).reshape(-1, model_width)
    gain_f, shift_f, bias_f, scale_f = (small[0:2], small[2:4], small[4:8], small[8:10])
    qkv_full = lax.all_gather(by_pair(w_qkv), IMG, axis=0, tiled=True)
    out_full = lax.all_gather(w_out, IMG, axis=0, tiled=True)
    up_full = lax.all_gather(w_up, IMG, axis=0, tiled=True)
    down_full = lax.all_gather(w_down, IMG, axis=0, tiled=True)

    tokens = jnp.stack([traded(tokens[slot]) for slot in range(images)])
    inputs = tokens.reshape(-1, model_width).astype(jnp.float32)
    normed_one, norm_one_pulls = [], []
    for slot in range(images):
        normed, pull = jax.vjp(norm_rows, tokens[slot].astype(jnp.float32), gain_f[0], shift_f[0])
        normed_one.append(normed.astype(jnp.bfloat16))
        norm_one_pulls.append(pull)
    rows_one = rows_of(jnp.concatenate(normed_one, axis=0))
    shift_qkv = jnp.concatenate([bias_f[0], jnp.zeros((model_width,), jnp.float32), bias_f[1]])
    shift_qkv = by_pair(shift_qkv[None])
    saved = []
    returned = []
    for slot in range(images):
        qkv = jnp.dot(normed_one[slot], qkv_full, preferred_element_type=jnp.float32)
        qkv = (qkv + shift_qkv).astype(jnp.bfloat16)
        spread = to_heads(qkv, pairs)
        mixed, log_total = attend(spread, key_bias[slot])
        saved.append((spread, key_bias[slot], log_total, mixed))
        returned.append(to_tokens(mixed))
    last, cotangent = lax.optimization_barrier((saved[-1][0], cotangent))
    saved[-1] = (last,) + saved[-1][1:]
    cotangent = traded(cotangent)
    attended = laid(returned)
    branch = jnp.dot(attended, out_full, preferred_element_type=jnp.float32) + bias_f[2]
    middle = inputs + scale_f[0] * branch
    normed_two, norm_two_pull = jax.vjp(norm_rows, middle, gain_f[1], shift_f[1])
    normed_two = normed_two.astype(jnp.bfloat16)
    up_proj = jnp.dot(normed_two, up_full, preferred_element_type=jnp.float32) + up_bias_f
    activated, gelu_slope = lax.optimization_barrier(gelu_and_slope(up_proj))
    grad_y = cotangent.reshape(-1, model_width).astype(jnp.float32) * live_rows
    grad_down = (grad_y * scale_f[1]).astype(jnp.bfloat16)
    grad_bias_down = jnp.sum(grad_down.astype(jnp.float32), axis=0)
    barrier = lax.optimization_barrier
    grad_down, grad_w_down = barrier((grad_down, product(activated, grad_down)))
    grad_w_down = lax.psum_scatter(grad_w_down, IMG, scatter_dimension=0, tiled=True)
    grad_act = jnp.dot(grad_down, down_full.T, preferred_element_type=jnp.float32)
    grad_up = (grad_act * gelu_slope).astype(jnp.bfloat16)
    grad_up_bias = jnp.sum(grad_up.astype(jnp.float32), axis=0)
    grad_up, grad_w_up = barrier((grad_up, product(normed_two, grad_up)))
    grad_w_up = lax.psum_scatter(grad_w_up, IMG, scatter_dimension=0, tiled=True)
    grad_normed_two = jnp.dot(grad_up, up_full.T, preferred_element_type=jnp.float32)
    grad_from_two, grad_gain_two, grad_shift_two = norm_two_pull(grad_normed_two)
    grad_middle = grad_y + grad_from_two
    grad_scale_one = jnp.sum(grad_middle * branch, axis=0)
    grad_branch = (grad_middle * scale_f[0]).astype(jnp.bfloat16)
    grad_bias_out = jnp.sum(grad_branch.astype(jnp.float32), axis=0)
    grad_attended = jnp.dot(grad_branch, out_full.T, preferred_element_type=jnp.float32).astype(
        jnp.bfloat16
    )
    grad_attended = grad_attended.reshape(images, local_rows, model_width)

    grad_w_out = products(rows_of(attended), grad_branch)
    grads_mixed = [to_heads(grad_attended[slot]) for slot in range(images)]
    grad_parts = []
    grad_w_qkv = []
    for pair in range(pairs):
        grad_slots = []
        for slot in range(images):
            spread, slot_bias, log_total, mixed = saved[slot]
            if pair == 0 and slot == 0:
                spread, grad_w_out = barrier((spread, grad_w_out))
            if pair and slot == images - 1:
                earlier = barrier((grad_parts[-1], grad_slots))
                grad_parts[-1] = laid(earlier[0])
                grad_slots = earlier[1]
                grad_w_qkv.append(products(rows_one, grad_parts[-1]))
                spread, grad_w_qkv[-1] = barrier((spread, grad_w_qkv[-1]))
            last = attend_back(pair, spread, slot_bias, log_total, mixed, grads_mixed[slot])
            if slot == images - 1 and pair == pairs - 1:
                last, activated = barrier((last, activated))
            grad_slots.append(to_tokens(last))
        grad_parts.append(grad_slots)
    grad_parts[-1] = laid(grad_parts[-1])
    grad_w_qkv.append(products(rows_one, grad_parts[-1]))
    grad_w_up = summed_seq(grad_w_up)
    grad_w_down = summed_seq(grad_w_down)
    grad_w_qkv[0] = [
        jnp.concatenate(both, axis=1) for both in zip(grad_w_qkv[0], grad_w_out, strict=True)
    ]
    grad_w_qkv = jnp.concatenate([owned(*both) for both in grad_w_qkv], axis=1)
    cut = 3 * seq_count * PAIR
    grad_w_out = grad_w_qkv[:, cut : cut + model_width]
    grad_w_qkv = jnp.concatenate([grad_w_qkv[:, :cut], grad_w_qkv[:, cut + model_width :]], axis=1)
    grad_w_qkv = by_kind(grad_w_qkv)

    down_proj = jnp.dot(activated, down_full, preferred_element_type=jnp.float32) + bias_f[3]
    result = (
        ((middle + scale_f[1] * down_proj) * live_rows).astype(jnp.bfloat16).reshape(tokens.shape)
    )
    result = traded(result)
    grad_scale_two = jnp.sum(grad_y * down_proj, axis=0)
    grad_inputs, grad_gain_one, grad_shift_one = [], 0.0, 0.0
    for slot in range(images):
        rows = slice(slot * local_rows, (slot + 1) * local_rows)
        grad_normed = 0.0
        for pair in range(pairs):
            cols = slice(pair * seq_count * 3 * PAIR, (pair + 1) * seq_count * 3 * PAIR)
            grad_normed += lax.dot_general(
                grad_parts[pair][rows],
                qkv_full[:, cols],
                (((1,), (1,)), ((), ())),
                preferred_element_type=jnp.float32,
            )
        grad_from_one, grad_gain, grad_shift = norm_one_pulls[slot](grad_normed)
        grad_inputs.append(traded((grad_middle[rows] + grad_from_one).astype(jnp.bfloat16)))
        grad_gain_one += grad_gain
        grad_shift_one += grad_shift
    grad_inputs = jnp.stack(grad_inputs)
    grad_bias_qkv = [jnp.sum(part.astype(jnp.float32), axis=0) for part in grad_parts]
    grad_bias_qkv = by_kind(jnp.concatenate(grad_bias_qkv)[None])[0]
    smalls = jnp.stack(
        [
            grad_gain_one,
            grad_gain_two,
            grad_shift_one,
            grad_shift_two,
            grad_bias_qkv[:model_width],
            grad_bias_qkv[2 * model_width :],
            grad_bias_out,
            grad_bias_down,
            grad_scale_one,
            grad_scale_two,
        ]
    )
    grad_up_bias = grad_up_bias.reshape(img_count, up_rows, shard).swapaxes(0, 1)
    smalls = jnp.concatenate([smalls, grad_up_bias.reshape(up_rows, model_width)], axis=0)
    smalls = summed(smalls)
    smalls = lax.dynamic_slice_in_dim(smalls, img_place * shard, shard, 1)
    return (
        result,
        grad_inputs,
        grad_w_qkv,
        grad_w_out,
        grad_w_up,
        grad_w_down,
        smalls[0:2],
        smalls[2:4],
        smalls[4:8],
        smalls[10:].reshape(-1),
        smalls[8:10],
    )


def solution(mesh):
    img_count, seq_count = mesh.devices.shape
    split = mesh.devices.reshape(img_count // 2, 2, 2, seq_count // 2)
    mesh = Mesh(split, IMG + SEQ)
    placed = (
        P(IMG, SEQ, None),
        P(IMG, SEQ, None),
        P(IMG, None),
        P(IMG),
        P(IMG, None),
        P(IMG, None),
        P(IMG, None),
        P(IMG, None),
        P(None, IMG),
        P(None, IMG),
        P(None, IMG),
        P(IMG),
        P(None, IMG),
    )
    return jax.shard_map(
        body,
        mesh=mesh,
        in_specs=placed,
        out_specs=(
            P(IMG, SEQ, None),
            P(IMG, SEQ, None),
            P(IMG, None),
            P(IMG, None),
            P(IMG, None),
            P(IMG, None),
            P(None, IMG),
            P(None, IMG),
            P(None, IMG),
            P(IMG),
            P(None, IMG),
        ),
        check_vma=False,
    )
```
